128 devices in a mesh: blk: 32 (over x_lo, z, y), rad: 4 (over x_hi, core).
Axes of the slice: x: 4 (x_hi: 2, x_lo: 2; x = x_hi * 2 + x_lo), y: 4, z: 4, core: 2. Of those that a mesh axis runs over, the one named last changes fastest.
Arguments:
- right_side: float32 [512, 2, 32, 4096], P(None, None, 'rad', 'blk'), may hold values from -6 to 6
- coefficient: float32 [512, 2, 32, 4096], P(None, None, 'rad', 'blk'), may hold values from 0.5 to 2
- geometry: float32 [3, 2, 32, 4096], P(None, None, 'rad', 'blk'), may hold values from 0.002 to 0.02
- interp: float32 [4, 64, 64], replicated, may hold values from -0.3 to 1.35
- face_map: int32 [32, 4096], P('rad', 'blk'), may hold values from 0 to 3
- offset: int32 [1], replicated, may hold values from 0 to 262143
Outputs:
- solution_field: float32 [512, 2, 32, 4096], P(None, None, 'rad', 'blk')
- residual: float32 [512, 2, 32, 4096], P(None, None, 'rad', 'blk')
The draws below stay inside these ranges and needn't reach their ends.
All inputs are finite; a program needn't handle non-finite values.
Results may differ from the reference program's by a relative error of at most 0.00011.
Values sent between devices are 32-bit elements; how exact they have to be, the bound alone decides.
A program may use at most 128 MiB of HBM per device.

```python
import math
import jax
import jax.numpy as jnp
from jax import lax

SIDES = 2
NMAT = 4
ITERS = 3
NODES = 512
NR = 32
NC = 4096


def draw_interp(key, part):
    key_noise = jax.random.fold_in(jax.random.fold_in(key, 17), 0)
    identity = jnp.eye(64, dtype=jnp.float32)
    jitter = jnp.clip(0.05 * jax.random.normal(key_noise, (NMAT, 64, 64), jnp.float32), -0.25, 0.25)
    scales = jnp.ones((NMAT, 1, 64), jnp.float32)
    return identity * scales + jitter


def with_ends(drawn, own_key, low, largest):
    longest = drawn.shape.index(max(drawn.shape))
    spots = []
    for shift in (0, 1):
        where = [jax.random.randint(jax.random.fold_in(own_key, axis), (), 0, length) for axis, length in enumerate(drawn.shape)]
        where[longest] = (where[longest] + shift) % drawn.shape[longest]
        spots.append(tuple(where))
    return drawn.at[spots[0]].set(low).at[spots[1]].set(largest)


def shard_levels(rng, dims, cuts, smallest, high):
    level = 1.0
    for position, shards_of in cuts:
        steps = jax.random.uniform(jax.random.fold_in(jax.random.fold_in(rng, 6), position), (shards_of,), jnp.float32, smallest / len(cuts), high / len(cuts))
        level = level * jnp.repeat(jnp.exp(steps), dims[position] // shards_of).reshape((-1,) + (1,) * (len(dims) - 1 - position))
    return level


def scatter_about(stream_key, extent, width, bound, cuts=(), kind=jnp.bfloat16):
    entries = jax.random.normal(stream_key, extent, jnp.float32) * width
    if len(cuts) > 0:
        entries = shard_levels(stream_key, extent, cuts, -0.22, 0.18) * entries
    return jnp.clip(entries, min=-bound, max=bound).astype(kind)


def setup_inputs(seed: int = 0) -> dict:
    streams_of = jax.random.split(jax.random.key(seed), 7)
    right_side = scatter_about(streams_of[0], (NODES, SIDES, NR, NC), 1.0, 6.0, ((2, 4), (3, 32)), jnp.float32)
    coefficient = jnp.clip(jnp.exp(math.log(2.0) - 1.3862944 * jax.random.uniform(streams_of[1], (NODES, SIDES, NR, NC), jnp.float32) ** shard_levels(streams_of[1], (NODES, SIDES, NR, NC), ((2, 4), (3, 32)), -0.2, 0.2)), 0.5, 2.0)
    geometry = jnp.clip(jnp.exp(math.log(0.02) - 2.30258502 * jax.random.uniform(streams_of[2], (3, SIDES, NR, NC), jnp.float32) ** shard_levels(streams_of[2], (3, SIDES, NR, NC), ((2, 4), (3, 32)), -0.2, 0.2)), 0.002, 0.02)
    interp = draw_interp(jax.random.fold_in(streams_of[6], 71), 0)
    face_map = with_ends(jax.random.randint(streams_of[4], (NR, NC), 0, NMAT), jax.random.fold_in(streams_of[4], 1), 0, NMAT - 1).astype(jnp.int32)
    offset = jax.random.randint(streams_of[5], (1,), 0, 64 * NC).astype(jnp.int32)
    return {"right_side": right_side, "coefficient": coefficient, "geometry": geometry, "interp": interp, "face_map": face_map, "offset": offset}


PENALTY = 1.0
HIGHEST = lax.Precision.HIGHEST


def spectral_derivative():
    counter = jnp.arange(8)
    points = -jnp.cos(jnp.pi * counter.astype(jnp.float32) / 7.0)
    endpoint = jnp.logical_or(counter == 0, counter == 7)
    weights = jnp.where(endpoint, 2.0, 1.0).astype(jnp.float32)
    parity = 1.0 - 2.0 * ((counter[:, None] + counter[None, :]) % 2).astype(jnp.float32)
    diagonal_mask = counter[:, None] == counter[None, :]
    spacing = jnp.where(diagonal_mask, 1.0, points[:, None] - points[None, :])
    off_terms = jnp.where(diagonal_mask, 0.0, weights[:, None] / weights[None, :] * parity / spacing)
    return off_terms - jnp.diag(jnp.sum(off_terms, axis=1))


def element_part(nodal, coefficient, geometry, derivative):
    flat_nodes = nodal.reshape(8, 8, 8, -1)
    factors = geometry.reshape(3, -1)
    result = coefficient.reshape(8, 8, 8, -1) * flat_nodes
    grad_one = jnp.einsum('ai,ijkx->ajkx', derivative, flat_nodes, precision=HIGHEST)
    result = result + jnp.einsum('ai,ajkx->ijkx', derivative, grad_one * factors[0], precision=HIGHEST)
    grad_two = jnp.einsum('bj,ijkx->ibkx', derivative, flat_nodes, precision=HIGHEST)
    result = result + jnp.einsum('bj,ibkx->ijkx', derivative, grad_two * factors[1], precision=HIGHEST)
    grad_three = jnp.einsum('ck,ijkx->ijcx', derivative, flat_nodes, precision=HIGHEST)
    result = result + jnp.einsum('ck,ijcx->ijkx', derivative, grad_three * factors[2], precision=HIGHEST)
    return result.reshape(nodal.shape)


def block_pick(interp, face_map):
    return (face_map[None] == jnp.arange(interp.shape[0])[:, None, None]).astype(jnp.float32)


def interface_jump(rotor_side, stator_side, interp, face_map):
    mapped = jnp.einsum('mpq,qrc->mprc', interp, rotor_side, precision=HIGHEST)
    picked = block_pick(interp, face_map)
    return jnp.sum(picked[:, None] * mapped, axis=0) - stator_side


def interface_back(face_jump, interp, face_map):
    mapped = jnp.einsum('mqp,qrc->mprc', interp, face_jump, precision=HIGHEST)
    picked = block_pick(interp, face_map)
    return jnp.sum(picked[:, None] * mapped, axis=0)


def operate(field_value, coefficient, geometry, interp, face_map, rotation, derivative):
    layers, radial, cycle_cells = field_value.shape[1], field_value.shape[2], field_value.shape[3]
    nodal = field_value.reshape(8, 8, 8, layers, radial, cycle_cells)
    result = element_part(nodal, coefficient, geometry, derivative)
    top_face = nodal[:, 7]
    bottom_face = nodal[:, 0]
    radial_jump = top_face[:, :, :, :-1] - bottom_face[:, :, :, 1:]
    result = result.at[:, 7, :, :, :-1, :].add(PENALTY * radial_jump)
    result = result.at[:, 0, :, :, 1:, :].add(-PENALTY * radial_jump)
    right_face = nodal[:, :, 7]
    left_face = nodal[:, :, 0]
    circ_jump = right_face - jnp.roll(left_face, -1, axis=4)
    result = result.at[:, :, 7].add(PENALTY * circ_jump)
    result = result.at[:, :, 0].add(-PENALTY * jnp.roll(circ_jump, 1, axis=4))
    rotor_face = nodal[7, :, :, 0].reshape(64, radial, cycle_cells)
    stator_face = nodal[0, :, :, 1].reshape(64, radial, cycle_cells)
    doubled = jnp.concatenate([rotor_face, rotor_face], axis=2)
    turned = lax.dynamic_slice_in_dim(doubled, (cycle_cells - rotation).astype(jnp.int32), cycle_cells, 2)
    face_jump = interface_jump(turned, stator_face, interp, face_map)
    back_terms = interface_back(face_jump, interp, face_map)
    doubled_back = jnp.concatenate([back_terms, back_terms], axis=2)
    returned = lax.dynamic_slice_in_dim(doubled_back, rotation.astype(jnp.int32), cycle_cells, 2)
    result = result.at[7, :, :, 0].add(PENALTY * returned.reshape(8, 8, radial, cycle_cells))
    result = result.at[0, :, :, 1].add(-PENALTY * face_jump.reshape(8, 8, radial, cycle_cells))
    return result.reshape(field_value.shape)


def reference(right_side, coefficient, geometry, interp, face_map, offset):
    derivative = spectral_derivative()
    cycle_total = right_side.shape[3]
    rotation = (offset[0].astype(jnp.int32) % cycle_total).astype(jnp.int32)
    solution_field = jnp.zeros_like(right_side)
    residual = right_side
    direction = right_side
    norm_now = jnp.sum(residual * residual)
    for iteration in range(ITERS):
        image = operate(direction, coefficient, geometry, interp, face_map, rotation, derivative)
        alpha = norm_now / jnp.sum(direction * image)
        solution_field = solution_field + alpha * direction
        residual = residual - alpha * image
        norm_next = jnp.sum(residual * residual)
        direction = residual + (norm_next / norm_now) * direction
        norm_now = norm_next
    return solution_field, residual
```

```python
import functools

import jax
import jax.numpy as jnp
import numpy as np
from jax import lax
from jax.experimental import pallas as pl
from jax.experimental.pallas import tpu as pltpu
from jax.sharding import PartitionSpec as P

ITERS = 3
MESH = pl.DeviceIdType.MESH
F32 = jnp.float32
BF16 = jnp.bfloat16


def stiffness_halves():
    n = np.arange(8)
    x = -np.cos(np.pi * n / 7.0)
    c = np.where((n == 0) | (n == 7), 2.0, 1.0)
    sign = 1.0 - 2.0 * ((n[:, None] + n[None, :]) % 2)
    gap = x[:, None] - x[None, :] + np.eye(8)
    d = (c[:, None] / c[None, :]) * sign / gap * (1.0 - np.eye(8))
    d = d - np.diag(d.sum(axis=1))
    k = d.T @ d
    mirror = k[:4, ::-1][:, :4]
    return 0.5 * (k[:4, :4] + mirror), 0.5 * (k[:4, :4] - mirror)


EVEN, ODD = stiffness_halves()


def line_apply(v):
    sums = [v[m] + v[7 - m] for m in range(4)]
    diffs = [v[m] - v[7 - m] for m in range(4)]
    out = [None] * 8
    for m in range(4):
        e = sums[0] * float(EVEN[m, 0])
        o = diffs[0] * float(ODD[m, 0])
        for n in range(1, 4):
            e = e + sums[n] * float(EVEN[m, n])
            o = o + diffs[n] * float(ODD[m, n])
        out[m] = e + o
        out[7 - m] = e - o
    return out


def split_rows(a):
    high = a.astype(BF16)
    low = (a - high.astype(F32)).astype(BF16)
    return jnp.concatenate([high, low, high, low], axis=0)


def split_columns(p):
    both = jnp.concatenate([p, p], axis=1)
    high = both.astype(BF16)
    low = (both - high.astype(F32)).astype(BF16)
    return jnp.concatenate([high, low], axis=1)


def choose(blocks, which):
    which = jnp.broadcast_to(which, (64, 128))
    out = blocks[0:64]
    for m in range(1, 4):
        out = jnp.where(which == float(m), blocks[64 * m : 64 * m + 64], out)
    return out


VMEM = pl.BlockSpec(memory_space=pltpu.VMEM)
SMEM = pl.BlockSpec(memory_space=pltpu.SMEM)


def struct(*shape):
    return jax.ShapeDtypeStruct(shape, F32)


def lanes():
    return lax.broadcasted_iota(jnp.int32, (8, 128), 1)


def rows():
    return lax.broadcasted_iota(jnp.int32, (8, 128), 0)


def pack_faces(read_rotor, read_stator, sa, sah, sb, sbh):
    lane = lanes()

    def body(n, carry):
        for read, full, half in ((read_rotor, sa, sah), (read_stator, sb, sbh)):
            one, two = read(n), read(n + 32)
            full[n] = one
            full[n + 32] = two
            half[0, n] = jnp.where(lane < 64, one, pltpu.roll(two, 64, 1))
            half[1, n] = jnp.where(lane < 64, pltpu.roll(one, 64, 1), two)
        return carry

    lax.fori_loop(0, 32, body, 0)


def pack_halos(read, hs, cs):
    lane = lanes()
    zero = jnp.zeros((8, 128), F32)

    def body(n, carry):
        upper, lower = carry
        side, i = n // 8, lax.rem(n, 8)
        for k in range(8):
            hs[0, n, pl.ds(k, 1), :] = read(64 * i + 56 + k, side)[7:8, :]
            hs[1, n, pl.ds(k, 1), :] = read(64 * i + k, side)[0:1, :]
        for j in range(8):
            place = 8 * n + j
            last = pltpu.roll(read(64 * i + 8 * j + 7, side), lax.rem(place + 1, 128), 1)
            first = pltpu.roll(read(64 * i + 8 * j, side), place, 1)
            upper = jnp.where(lane == place, last, upper)
            lower = jnp.where(lane == place, first, lower)
        return upper, lower

    upper, lower = lax.fori_loop(0, 16, body, (zero, zero))
    cs[0] = upper
    cs[1] = lower


def turn(main, near, by):
    lane = lanes()
    first = jnp.where(by > 0, 128 - by, 0)
    end = jnp.where(by > 0, 128, -by)
    missing = jnp.logical_and(lane >= first, lane < end)
    picked = jnp.where(missing, near, main)
    return pltpu.roll(picked, lax.rem(by + 128, 128), 1)


PACKED = [
    struct(64, 8, 128),
    struct(2, 32, 8, 128),
    struct(65, 8, 128),
    struct(2, 33, 8, 128),
    struct(2, 16, 8, 128),
    struct(2, 8, 128),
]


def opening(rhs, face_map, interp, sa, sah, sb, sbh, hs, cs, weights):
    pack_faces(lambda n: rhs[n + 448, 0], lambda n: rhs[n, 1], sa, sah, sb, sbh)
    which = face_map[...].astype(F32)
    sb[64] = which
    sbh[0, 32] = which
    sbh[1, 32] = which
    pack_halos(lambda n, side: rhs[n, side], hs, cs)
    blocks = interp[...]
    weights[0] = split_columns(blocks.reshape(256, 64))
    turned = jnp.concatenate(
        [
            jnp.concatenate([blocks[0], blocks[1]], axis=1).T,
            jnp.concatenate([blocks[2], blocks[3]], axis=1).T,
        ],
        axis=0,
    )
    weights[1] = split_columns(turned)


def opened(right_side, face_map, interp):
    return pl.pallas_call(
        opening,
        out_shape=PACKED + [jax.ShapeDtypeStruct((2, 256, 256), BF16)],
        in_specs=[VMEM] * 3,
        out_specs=[VMEM] * 7,
        compiler_params=pltpu.CompilerParams(vmem_limit_bytes=32 * 1024 * 1024),
    )(right_side, face_map, interp)


def exchange(nb, nr, hop, *refs):
    sa, sah, sb, sbh, hs, cs, ra, rah, rb, rbh, hrecv, crecv, send_sem, recv_sem = refs
    blk = lax.axis_index("blk")
    rad = lax.axis_index("rad")

    def along(by):
        return {"blk": lax.rem(blk + by + 2 * nb, nb), "rad": rad}

    def across(by):
        return {"blk": blk, "rad": lax.rem(rad + by + nr, nr)}

    plan = []
    for src, half, dst, dhalf, way in ((sa, sah, ra, rah, 1), (sb, sbh, rb, rbh, -1)):
        for source, target, by in (
            (src, dst, way * hop),
            (half.at[0], dhalf.at[0], way * hop - 1),
            (half.at[1], dhalf.at[1], way * hop + 1),
        ):
            plan.append((source, target, along(by) if by % nb else None))
    plan += [
        (hs.at[0], hrecv.at[0], across(1)),
        (hs.at[1], hrecv.at[1], across(-1)),
        (cs.at[0], crecv.at[0], along(1)),
        (cs.at[1], crecv.at[1], along(-1)),
    ]
    peers = [peer for _, _, peer in plan if peer is not None]
    barrier = pltpu.get_barrier_semaphore()
    for peer in peers:
        pl.semaphore_signal(barrier, inc=1, device_id=peer, device_id_type=MESH)
    pl.semaphore_wait(barrier, len(peers))
    copies = []
    for n, (source, target, peer) in enumerate(plan):
        if peer is None:
            copy = pltpu.make_async_copy(source, target, recv_sem.at[n])
        else:
            copy = pltpu.make_async_remote_copy(
                source,
                target,
                send_sem.at[n],
                recv_sem.at[n],
                device_id=peer,
                device_id_type=MESH,
            )
        copy.start()
        copies.append(copy)
    for copy in copies:
        copy.wait()


def exchanged(nb, nr, hop, *packed):
    return pl.pallas_call(
        functools.partial(exchange, nb, nr, hop),
        out_shape=PACKED,
        in_specs=[VMEM] * 6,
        out_specs=[VMEM] * 6,
        scratch_shapes=[pltpu.SemaphoreType.DMA((10,)), pltpu.SemaphoreType.DMA((10,))],
        compiler_params=pltpu.CompilerParams(collective_id=hop, has_side_effects=True),
    )(*packed)


def reduce_kernel(nb, nr, part, scal, source, one, two, send_sem, recv_sem):
    blk = lax.axis_index("blk")
    rad = lax.axis_index("rad")

    def plane_peer(d):
        return {"blk": (blk // 16) * 16 + lax.rem(lax.rem(blk, 16) + d, 16), "rad": rad}

    def line_peer(d):
        place = lax.rem((blk // 16) * nr + rad + d, 2 * nr)
        return {"blk": (place // nr) * 16 + lax.rem(blk, 16), "rad": lax.rem(place, nr)}

    stages = (
        (16, lax.rem(blk, 16), plane_peer, one),
        (2 * nr, (blk // 16) * nr + rad, line_peer, two),
    )
    barrier = pltpu.get_barrier_semaphore()
    for count, _, peer, _ in stages:
        for d in range(1, count):
            pl.semaphore_signal(barrier, inc=1, device_id=peer(d), device_id_type=MESH)
    pl.semaphore_wait(barrier, 14 + 2 * nr)
    tile = part[...]
    for stage, (count, place, peer, buf) in enumerate(stages):
        source[stage] = tile
        buf[place] = tile
        for d in range(1, count):
            pltpu.make_async_remote_copy(
                source.at[stage],
                buf.at[place],
                send_sem.at[stage],
                recv_sem.at[stage],
                device_id=peer(d),
                device_id_type=MESH,
            ).start()
        whole = buf.at[pl.ds(0, count - 1)]
        pltpu.make_async_copy(whole, whole, recv_sem.at[stage]).wait()
        tile = buf[0]
        for n in range(1, count):
            tile = tile + buf[n]
        pltpu.make_async_copy(whole, whole, send_sem.at[stage]).wait()
    totals = jnp.sum(tile, axis=1, keepdims=True)
    pq, rq, qq, rr = [jnp.broadcast_to(totals[n : n + 1], (8, 128)) for n in range(4)]
    alpha = rr / pq
    fresh = rr - 2.0 * alpha * rq + alpha * alpha * qq
    scal[0] = alpha
    scal[1] = fresh / rr


def reduced(nb, nr, part):
    return pl.pallas_call(
        functools.partial(reduce_kernel, nb, nr),
        out_shape=struct(2, 8, 128),
        in_specs=[VMEM],
        out_specs=VMEM,
        scratch_shapes=[
            pltpu.VMEM((2, 8, 128), F32),
            pltpu.VMEM((16, 8, 128), F32),
            pltpu.VMEM((2 * nr, 8, 128), F32),
            pltpu.SemaphoreType.DMA((2,)),
            pltpu.SemaphoreType.DMA((2,)),
        ],
        compiler_params=pltpu.CompilerParams(collective_id=nb, has_side_effects=True),
    )(part)


def step(first, last, nr, *refs):
    refs = list(refs)
    take = lambda n: [refs.pop(0) for _ in range(n)]
    offset, rold, cf, geom, weights = take(5)
    ra, rah, rb, rbh, hrecv, crecv = take(6)
    if first:
        (face_map,) = take(1)
        alpha = beta = None
    else:
        scal, pold, qold, maps = take(4)
        olds = take(8)
        alpha, beta = scal[0], scal[1]
    p, q, part = take(3)
    if not first:
        (r,) = take(1)
    else:
        r = rold
        (maps,) = take(1)
    news = take(8)
    if not last:
        packed = take(6)
    rad = lax.axis_index("rad")
    lane, row = lanes(), rows()
    zero = jnp.zeros((8, 128), F32)
    shift = lax.rem(offset[0] + 64, 128) - 64
    if first:
        maps[0] = face_map[...].astype(F32)
        maps[1] = turn(rb[64], jnp.where(lane < 64, rbh[0, 32], rbh[1, 32]), -shift)
    a_res, a_dir, b_res, b_dir, h_res, h_dir, c_res, c_dir = news

    def refresh(slot, place, fresh):
        res, ahead = news[slot], news[slot + 1]
        if first:
            res[place] = fresh
            ahead[place] = fresh
        else:
            value = olds[slot][place] - alpha * fresh
            res[place] = value
            ahead[place] = value + beta * olds[slot + 1][place]

    def columns(t, total):
        for s in range(2):
            v = []
            for i in range(8):
                n = 64 * i + t
                if first:
                    value = rold[n, s]
                    ahead = value
                else:
                    value = rold[n, s] - alpha * qold[n, s]
                    r[n, s] = value
                    ahead = value + beta * pold[n, s]
                total = total + value * value
                p[n, s] = ahead
                v.append(ahead)
            g = geom[0, s]
            for i, value in enumerate(line_apply(v)):
                q[64 * i + t, s] = cf[64 * i + t, s] * v[i] + g * value
        return total

    rr = lax.fori_loop(0, 64, columns, zero)

    def halo_step(n, carry):
        for side in range(2):
            refresh(4, (side, n), hrecv[side, n])
        return carry

    lax.fori_loop(0, 16, halo_step, 0)
    for side in range(2):
        refresh(6, side, crecv[side])

    def face_step(n, carry):
        for main, half, slot, by in ((ra, rah, 0, shift), (rb, rbh, 2, -shift)):
            low, high = half[0, n], half[1, n]
            mixed = pltpu.roll(jnp.where(lane < 64, high, low), 64, 1)
            nears = (jnp.where(lane < 64, low, mixed), jnp.where(lane < 64, mixed, high))
            for place, near in zip((n, n + 32), nears):
                refresh(slot, place, turn(main[place], near, by))
        return carry

    lax.fori_loop(0, 32, face_step, 0)

    def pair(half, carry):
        jumps = []
        here = []
        for u in range(2):
            rr_ = 2 * half + u
            own = p[pl.ds(448, 64), 0, rr_, :]
            over = a_dir[:, rr_, :]
            mapped = jnp.dot(
                weights[0],
                split_rows(jnp.concatenate([own, over], axis=1)),
                preferred_element_type=F32,
            )
            mine = maps[1, pl.ds(rr_, 1), :]
            theirs = maps[0, pl.ds(rr_, 1), :]
            jumps.append(choose(mapped[:, :128], mine) - b_dir[:, rr_, :])
            here.append(mine)
            jump = choose(mapped[:, 128:], theirs) - p[pl.ds(0, 64), 1, rr_, :]
            q[pl.ds(0, 64), 1, rr_, :] = q[pl.ds(0, 64), 1, rr_, :] - jump
        back = jnp.dot(
            weights[1],
            split_rows(jnp.concatenate(jumps, axis=1)),
            preferred_element_type=F32,
        )
        for u in range(2):
            rr_ = 2 * half + u
            added = choose(back[:, 128 * u : 128 * u + 128], here[u])
            q[pl.ds(448, 64), 0, rr_, :] = q[pl.ds(448, 64), 0, rr_, :] + added
        return carry

    lax.fori_loop(0, 4, pair, 0)

    upper_open = row < jnp.where(rad < nr - 1, 8, 7)
    lower_open = row >= jnp.where(rad > 0, 0, 1)

    def plane(t, sums):
        s, i = t // 8, lax.rem(t, 8)
        base = 64 * i
        g_r, g_c = geom[1, s], geom[2, s]
        after, before = c_dir[1], c_dir[0]
        for j in range(8):
            v = [p[base + 8 * j + k, s] for k in range(8)]
            w = line_apply(v)
            place = 64 * s + 8 * i + j
            nxt = jnp.where(
                lane == 127, pltpu.roll(after, 127 - place, 1), pltpu.roll(v[0], 127, 1)
            )
            prv = jnp.where(
                lane == 0,
                pltpu.roll(before, lax.rem(128 - place, 128), 1),
                pltpu.roll(v[7], 1, 1),
            )
            for k in range(8):
                value = q[base + 8 * j + k, s] + g_c * w[k]
                if k == 7:
                    value = value + (v[7] - nxt)
                if k == 0:
                    value = value - (prv - v[0])
                q[base + 8 * j + k, s] = value
        pq, rq, qq = zero, zero, zero
        for k in range(8):
            v = [p[base + 8 * j + k, s] for j in range(8)]
            w = line_apply(v)
            above = h_dir[1, 8 * s + i, pl.ds(k, 1), :]
            below = h_dir[0, 8 * s + i, pl.ds(k, 1), :]
            nxt = jnp.where(row == 7, above, pltpu.roll(v[0], 7, 0))
            prv = jnp.where(row == 0, below, pltpu.roll(v[7], 1, 0))
            for j in range(8):
                n = base + 8 * j + k
                value = q[n, s] + g_r * w[j]
                if j == 7:
                    value = value + jnp.where(upper_open, v[7] - nxt, 0.0)
                if j == 0:
                    value = value - jnp.where(lower_open, prv - v[0], 0.0)
                q[n, s] = value
                pq = pq + v[j] * value
                rq = rq + r[n, s] * value
                qq = qq + value * value
        return sums[0] + pq, sums[1] + rq, sums[2] + qq

    pq, rq, qq = lax.fori_loop(0, 16, plane, (zero, zero, zero))
    tile = zero
    for n, one in enumerate((pq, rq, qq, rr)):
        tile = jnp.where(row == n, jnp.sum(one, axis=0, keepdims=True), tile)
    part[...] = tile
    if not last:
        sa, sah, sb, sbh, hs, cs = packed
        pack_faces(lambda n: q[n + 448, 0], lambda n: q[n, 1], sa, sah, sb, sbh)
        for ref in (sb.at[64], sbh.at[0, 32], sbh.at[1, 32]):
            ref[...] = zero
        pack_halos(lambda n, side: q[n, side], hs, cs)


FACES = [struct(64, 8, 128)] * 4 + [struct(2, 16, 8, 128)] * 2 + [struct(2, 8, 128)] * 2


def stepped(first, last, nr, offset, rold, cf, geom, weights, received, *rest):
    field = struct(*rold.shape)
    outs = [field, field, struct(8, 128)]
    outs += [struct(2, 8, 128)] if first else [field]
    outs += FACES
    if not last:
        outs += PACKED
    args = [offset, rold, cf, geom, weights, *received, *rest]
    aliases = {}
    if not first:
        aliases = {12: 0, 13: 1}
        aliases.update({15 + n: 4 + n for n in range(8)})
    return pl.pallas_call(
        functools.partial(step, first, last, nr),
        out_shape=outs,
        in_specs=[SMEM] + [VMEM] * (len(args) - 1),
        out_specs=[VMEM] * len(outs),
        input_output_aliases=aliases,
        compiler_params=pltpu.CompilerParams(vmem_limit_bytes=LIMIT * 1024 * 1024),
    )(*args)


LIMIT = 48

def finish(r0, r1, r2, q, c, x_out, r_out):
    c0, c1, c2 = c[0][None, None], c[1][None, None], c[2][None, None]
    last = r2[...]
    x_out[...] = c0 * r0[...] + c1 * r1[...] + c2 * last
    r_out[...] = last - c2 * q[...]


def finished(r0, r1, r2, q, c):
    points = 32
    block = pl.BlockSpec((points,) + r0.shape[1:], lambda n: (n, 0, 0, 0))
    return pl.pallas_call(
        finish,
        grid=(r0.shape[0] // points,),
        out_shape=[jax.ShapeDtypeStruct(r0.shape, F32)] * 2,
        in_specs=[block] * 4 + [pl.BlockSpec(c.shape, lambda n: (0, 0, 0))],
        out_specs=[block] * 2,
        compiler_params=pltpu.CompilerParams(vmem_limit_bytes=32 * 1024 * 1024),
    )(r0, r1, r2, q, c)


HOPS = None


def on_device(nb, nr, right_side, coefficient, geometry, interp, face_map, offset):
    cells = nb * right_side.shape[3]
    rotation = lax.rem(offset[0], cells)
    hops = lax.rem((rotation + 64) // 128, nb)

    def swap(packed):
        if HOPS is None:
            branches = [functools.partial(exchanged, nb, nr, hop) for hop in range(nb)]
            return lax.switch(hops, branches, *packed)
        return exchanged(nb, nr, HOPS, *packed)

    *packed, weights = opened(right_side, face_map, interp)
    got = swap(packed)
    p, q, part, maps, *rest = stepped(
        True, False, nr, offset, right_side, coefficient, geometry, weights, got, face_map
    )
    states, packed = rest[:8], rest[8:]
    residuals = [right_side]
    factors = []
    for it in range(1, ITERS):
        factors.append(reduced(nb, nr, part))
        got = swap(packed)
        p, q, part, r, *rest = stepped(
            False,
            it == ITERS - 1,
            nr,
            offset,
            residuals[-1],
            coefficient,
            geometry,
            weights,
            got,
            factors[-1],
            p,
            q,
            maps,
            *states,
        )
        states, packed = rest[:8], rest[8:]
        residuals.append(r)
    factors.append(reduced(nb, nr, part))
    (a0, b0), (a1, b1), (a2, _) = factors
    one = a1 + b1 * a2
    weighed = jnp.stack([a0 + b0 * one, one, a2])
    return tuple(finished(*residuals, q, weighed))


def solution(mesh):
    nb, nr = mesh.shape["blk"], mesh.shape["rad"]
    field = P(None, None, "rad", "blk")
    return jax.shard_map(
        functools.partial(on_device, nb, nr),
        mesh=mesh,
        in_specs=(field, field, field, P(), P("rad", "blk"), P()),
        out_specs=(field, field),
        check_vma=False,
    )
```

```python
import functools

import jax
import jax.numpy as jnp
import numpy as np
from jax import lax
from jax.experimental import pallas as pl
from jax.experimental.pallas import tpu as pltpu
from jax.sharding import PartitionSpec as P

ITERS = 3
MESH = pl.DeviceIdType.MESH
F32 = jnp.float32
BF16 = jnp.bfloat16


def stiffness_halves():
    n = np.arange(8)
    x = -np.cos(np.pi * n / 7.0)
    c = np.where((n == 0) | (n == 7), 2.0, 1.0)
    sign = 1.0 - 2.0 * ((n[:, None] + n[None, :]) % 2)
    gap = x[:, None] - x[None, :] + np.eye(8)
    d = (c[:, None] / c[None, :]) * sign / gap * (1.0 - np.eye(8))
    d = d - np.diag(d.sum(axis=1))
    k = d.T @ d
    mirror = k[:4, ::-1][:, :4]
    return 0.5 * (k[:4, :4] + mirror), 0.5 * (k[:4, :4] - mirror)


EVEN, ODD = stiffness_halves()


def line_apply(v):
    sums = [v[m] + v[7 - m] for m in range(4)]
    diffs = [v[m] - v[7 - m] for m in range(4)]
    out = [None] * 8
    for m in range(4):
        e = sums[0] * float(EVEN[m, 0])
        o = diffs[0] * float(ODD[m, 0])
        for n in range(1, 4):
            e = e + sums[n] * float(EVEN[m, n])
            o = o + diffs[n] * float(ODD[m, n])
        out[m] = e + o
        out[7 - m] = e - o
    return out


def split_rows(a):
    high = a.astype(BF16)
    low = (a - high.astype(F32)).astype(BF16)
    return jnp.concatenate([high, low, high, low], axis=0)


def split_columns(p):
    both = jnp.concatenate([p, p], axis=1)
    high = both.astype(BF16)
    low = (both - high.astype(F32)).astype(BF16)
    return jnp.concatenate([high, low], axis=1)


def choose(blocks, which):
    which = jnp.broadcast_to(which, (64, 128))
    out = blocks[0:64]
    for m in range(1, 4):
        out = jnp.where(which == float(m), blocks[64 * m : 64 * m + 64], out)
    return out


VMEM = pl.BlockSpec(memory_space=pltpu.VMEM)
SMEM = pl.BlockSpec(memory_space=pltpu.SMEM)
EDGE = pl.BlockSpec(memory_space=pl.ANY)


def struct(*shape):
    return jax.ShapeDtypeStruct(shape, F32)


def lanes():
    return lax.broadcasted_iota(jnp.int32, (8, 128), 1)


def rows():
    return lax.broadcasted_iota(jnp.int32, (8, 128), 0)


def pack_face(read, full, half):
    lane = lanes()

    def body(n, carry):
        one, two = read(n), read(n + 32)
        full[n] = one
        full[n + 32] = two
        half[0][n] = jnp.where(lane < 64, one, pltpu.roll(two, 64, 1))
        half[1][n] = jnp.where(lane < 64, pltpu.roll(one, 64, 1), two)
        return carry

    lax.fori_loop(0, 32, body, 0)


def pack_halos(read, hs, cs):
    lane = lanes()
    zero = jnp.zeros((8, 128), F32)

    def body(n, carry):
        upper, lower = carry
        side, i = n // 8, lax.rem(n, 8)
        for k in range(8):
            hs[0][n, pl.ds(k, 1), :] = read(64 * i + 56 + k, side)[7:8, :]
            hs[1][n, pl.ds(k, 1), :] = read(64 * i + k, side)[0:1, :]
        for j in range(8):
            place = 8 * n + j
            last = pltpu.roll(read(64 * i + 8 * j + 7, side), lax.rem(place + 1, 128), 1)
            first = pltpu.roll(read(64 * i + 8 * j, side), place, 1)
            upper = jnp.where(lane == place, last, upper)
            lower = jnp.where(lane == place, first, lower)
        return upper, lower

    upper, lower = lax.fori_loop(0, 16, body, (zero, zero))
    cs[0][0] = upper
    cs[1][0] = lower


def turn(main, near, by):
    lane = lanes()
    first = jnp.where(by > 0, 128 - by, 0)
    end = jnp.where(by > 0, 128, -by)
    missing = jnp.logical_and(lane >= first, lane < end)
    picked = jnp.where(missing, near, main)
    return pltpu.roll(picked, lax.rem(by + 128, 128), 1)


SENT = 296
KEPT = 328


def sent_parts(ref):
    part = lambda first, count: ref.at[pl.ds(first, count)]
    return (
        part(0, 64),
        (part(64, 32), part(96, 32)),
        part(128, 65),
        (part(193, 33), part(226, 33)),
        (part(259, 16), part(275, 16)),
        (part(291, 1), part(292, 1)),
    )


def kept_parts(ref):
    part = lambda first, count: ref.at[pl.ds(first, count)]
    return [part(64 * n, 64) for n in range(4)] + [
        part(256, 32),
        part(288, 32),
        part(320, 2),
        part(322, 2),
    ]


def opening(rhs, face_map, interp, sent, weights):
    sa, sah, sb, sbh, hs, cs = sent_parts(sent)
    pack_face(lambda n: rhs[7, n, 0], sa, sah)
    pack_face(lambda n: rhs[0, n, 1], sb, sbh)
    which = face_map[...].astype(F32)
    sb[64] = which
    sbh[0][32] = which
    sbh[1][32] = which
    pack_halos(lambda n, side: rhs[n // 64, lax.rem(n, 64), side], hs, cs)
    blocks = interp[...]
    weights[0] = split_columns(blocks.reshape(256, 64))
    turned = jnp.concatenate(
        [
            jnp.concatenate([blocks[0], blocks[1]], axis=1).T,
            jnp.concatenate([blocks[2], blocks[3]], axis=1).T,
        ],
        axis=0,
    )
    weights[1] = split_columns(turned)


def opened(right_side, face_map, interp):
    return pl.pallas_call(
        opening,
        out_shape=[struct(SENT, 8, 128), jax.ShapeDtypeStruct((2, 256, 256), BF16)],
        in_specs=[VMEM] * 3,
        out_specs=[VMEM] * 2,
        compiler_params=pltpu.CompilerParams(vmem_limit_bytes=LIMIT * 1024 * 1024),
    )(right_side, face_map, interp)


def exchange(nb, nr, hop, up, own_barrier, sent, got, send_sem, recv_sem):
    blk = lax.axis_index("blk")
    rad = lax.axis_index("rad")

    def along(by):
        return {"blk": lax.rem(blk + by + 2 * nb, nb), "rad": rad}

    def across(by):
        return {"blk": blk, "rad": lax.rem(rad + by + nr, nr)}

    sa, sah, sb, sbh, hs, cs = sent_parts(sent)
    ra, rah, rb, rbh, hrecv, crecv = sent_parts(got)
    plan = []
    for src, half, dst, dhalf, way, high in (
        (sa, sah, ra, rah, 1, up),
        (sb, sbh, rb, rbh, -1, not up),
    ):
        beyond = way * hop + (1 if high else -1)
        for source, target, by in (
            (src, dst, way * hop),
            (half[int(high)], dhalf[int(high)], beyond),
        ):
            plan.append((source, target, along(by) if by % nb else None))
    plan += [
        (hs[0], hrecv[0], across(1)),
        (hs[1], hrecv[1], across(-1)),
        (cs[0], crecv[0], along(1)),
        (cs[1], crecv[1], along(-1)),
    ]
    peers = [peer for _, _, peer in plan if peer is not None]
    if own_barrier:
        barrier = pltpu.get_barrier_semaphore()
        for peer in peers:
            pl.semaphore_signal(barrier, inc=1, device_id=peer, device_id_type=MESH)
        pl.semaphore_wait(barrier, len(peers))
    copies = []
    for n, (source, target, peer) in enumerate(plan):
        if peer is None:
            copy = pltpu.make_async_copy(source, target, recv_sem.at[n])
        else:
            copy = pltpu.make_async_remote_copy(
                source,
                target,
                send_sem.at[n],
                recv_sem.at[n],
                device_id=peer,
                device_id_type=MESH,
            )
        copy.start()
        copies.append(copy)
    for copy in copies:
        copy.wait()


def exchanged(nb, nr, hop, up, sent):
    number = 2 * hop + int(up)
    own_barrier = number < 2 * nb - 1
    return pl.pallas_call(
        functools.partial(exchange, nb, nr, hop, up, own_barrier),
        out_shape=struct(*sent.shape),
        in_specs=[EDGE],
        out_specs=EDGE,
        scratch_shapes=[pltpu.SemaphoreType.DMA((8,)), pltpu.SemaphoreType.DMA((8,))],
        compiler_params=pltpu.CompilerParams(
            collective_id=number if own_barrier else None,
            has_side_effects=True,
            vmem_limit_bytes=LIMIT * 1024 * 1024,
        ),
    )(sent)


def reduce_kernel(nb, nr, part, scal, source, one, two, send_sem, recv_sem):
    blk = lax.axis_index("blk")
    rad = lax.axis_index("rad")

    def plane_peer(d):
        return {"blk": (blk // 16) * 16 + lax.rem(lax.rem(blk, 16) + d, 16), "rad": rad}

    def line_peer(d):
        place = lax.rem((blk // 16) * nr + rad + d, 2 * nr)
        return {"blk": (place // nr) * 16 + lax.rem(blk, 16), "rad": lax.rem(place, nr)}

    stages = (
        (16, lax.rem(blk, 16), plane_peer, one),
        (2 * nr, (blk // 16) * nr + rad, line_peer, two),
    )
    barrier = pltpu.get_barrier_semaphore()
    for count, _, peer, _ in stages:
        for d in range(1, count):
            pl.semaphore_signal(barrier, inc=1, device_id=peer(d), device_id_type=MESH)
    pl.semaphore_wait(barrier, 14 + 2 * nr)
    tile = part[...]
    for stage, (count, place, peer, buf) in enumerate(stages):
        source[stage] = tile
        buf[place] = tile
        for d in range(1, count):
            pltpu.make_async_remote_copy(
                source.at[stage],
                buf.at[place],
                send_sem.at[stage],
                recv_sem.at[stage],
                device_id=peer(d),
                device_id_type=MESH,
            ).start()
        whole = buf.at[pl.ds(0, count - 1)]
        pltpu.make_async_copy(whole, whole, recv_sem.at[stage]).wait()
        tile = buf[0]
        for n in range(1, count):
            tile = tile + buf[n]
        pltpu.make_async_copy(whole, whole, send_sem.at[stage]).wait()
    totals = jnp.sum(tile, axis=1, keepdims=True)
    pq, rq, qq, rr = [jnp.broadcast_to(totals[n : n + 1], (8, 128)) for n in range(4)]
    alpha = rr / pq
    fresh = rr - 2.0 * alpha * rq + alpha * alpha * qq
    scal[0] = alpha
    scal[1] = fresh / rr


def reduced(nb, nr, part):
    return pl.pallas_call(
        functools.partial(reduce_kernel, nb, nr),
        out_shape=struct(2, 8, 128),
        in_specs=[VMEM],
        out_specs=VMEM,
        scratch_shapes=[
            pltpu.VMEM((2, 8, 128), F32),
            pltpu.VMEM((16, 8, 128), F32),
            pltpu.VMEM((2 * nr, 8, 128), F32),
            pltpu.SemaphoreType.DMA((2,)),
            pltpu.SemaphoreType.DMA((2,)),
        ],
        compiler_params=pltpu.CompilerParams(
            collective_id=2 * nb - 1, has_side_effects=True, vmem_limit_bytes=LIMIT * 1024 * 1024
        ),
    )(part)


CHUNKS = 4
PLANES = 4


def step(first, last, nr, *refs):
    refs = list(refs)
    take = lambda n: [refs.pop(0) for _ in range(n)]
    offset, rold, cf, geom, weights = take(5)
    (got,) = take(1)
    ra, rah, rb, rbh, hrecv, crecv = sent_parts(got)
    if first:
        (face_map,) = take(1)
        alpha = beta = None
    else:
        scal, pold, qold, maps = take(4)
        olds = kept_parts(take(1)[0])
        alpha, beta = scal[0], scal[1]
    qout, part = take(2)
    if first:
        (maps,) = take(1)
    else:
        (rout,) = take(1)
    if not (first or last):
        (pout,) = take(1)
    news = kept_parts(take(1)[0])
    if not last:
        sa, sah, sb, sbh, hs, cs = sent_parts(take(1)[0])
    ps, qs, sums = take(3)
    rs = ps if first else take(1)[0]
    t = pl.program_id(0)
    rad = lax.axis_index("rad")
    lane, row = lanes(), rows()
    zero = jnp.zeros((8, 128), F32)
    shift = lax.rem(offset[0] + 64, 128) - 64
    a_res, a_dir, b_res, b_dir, h_res, h_dir, c_res, c_dir = news
    span = 64 // CHUNKS
    thick = 8 // PLANES

    @pl.when(t == 0)
    def _():
        for n in range(4):
            sums[n] = zero
        if first:
            maps[0] = face_map[...].astype(F32)
            maps[1] = turn(rb[64], jnp.where(lane < 64, rbh[0][32], rbh[1][32]), -shift)

    def refresh(slot, place, fresh):
        res, ahead = news[slot], news[slot + 1]
        if first:
            res[place] = fresh
            ahead[place] = fresh
        else:
            value = olds[slot][place] - alpha * fresh
            res[place] = value
            ahead[place] = value + beta * olds[slot + 1][place]

    def columns(u, total):
        line = span * t + u
        for s in range(2):
            r = [rold[i, u, s] for i in range(8)]
            if first:
                v = r
            else:
                q = [qold[i, u, s] for i in range(8)]
                p = [pold[i, u, s] for i in range(8)]
                r = [r[i] - alpha * q[i] for i in range(8)]
                v = [r[i] + beta * p[i] for i in range(8)]
            c = [cf[i, u, s] for i in range(8)]
            g = geom[0, s]
            w = line_apply(v)
            squares = [x * x for x in r]
            squares = [squares[n] + squares[n + 4] for n in range(4)]
            total = total + ((squares[0] + squares[1]) + (squares[2] + squares[3]))
            for i in range(8):
                n = 64 * i + line
                ps[n, s] = v[i]
                if not first:
                    rs[n, s] = r[i]
                    rout[i, u, s] = r[i]
                    if not last:
                        pout[i, u, s] = v[i]
                qs[n, s] = c[i] * v[i] + g * w[i]
        return total

    @pl.when(t < CHUNKS)
    def _():
        sums[3] = sums[3] + lax.fori_loop(0, span, columns, zero)

    def halo_step(n, carry):
        for side in range(2):
            refresh(4, 16 * side + n, hrecv[side][n])
        return carry

    def face_step(n, carry):
        for main, half, slot, by in ((ra, rah, 0, shift), (rb, rbh, 2, -shift)):
            low, high = half[0][n], half[1][n]
            mixed = pltpu.roll(jnp.where(lane < 64, high, low), 64, 1)
            nears = (jnp.where(lane < 64, low, mixed), jnp.where(lane < 64, mixed, high))
            for place, near in zip((n, n + 32), nears):
                refresh(slot, place, turn(main[place], near, by))
        return carry

    @pl.when(t == 0)
    def _():
        lax.fori_loop(0, 16, halo_step, 0)
        for side in range(2):
            refresh(6, side, crecv[side][0])
        lax.fori_loop(0, 32, face_step, 0)

    def pair(half, carry):
        jumps = []
        here = []
        for u in range(2):
            r = 2 * half + u
            own = ps[pl.ds(448, 64), 0, r, :]
            over = a_dir[:, r, :]
            mapped = jnp.dot(
                weights[0],
                split_rows(jnp.concatenate([own, over], axis=1)),
                preferred_element_type=F32,
            )
            mine = maps[1, pl.ds(r, 1), :]
            theirs = maps[0, pl.ds(r, 1), :]
            jumps.append(choose(mapped[:, :128], mine) - b_dir[:, r, :])
            here.append(mine)
            jump = choose(mapped[:, 128:], theirs) - ps[pl.ds(0, 64), 1, r, :]
            qs[pl.ds(0, 64), 1, r, :] = qs[pl.ds(0, 64), 1, r, :] - jump
        back = jnp.dot(
            weights[1],
            split_rows(jnp.concatenate(jumps, axis=1)),
            preferred_element_type=F32,
        )
        for u in range(2):
            r = 2 * half + u
            added = choose(back[:, 128 * u : 128 * u + 128], here[u])
            qs[pl.ds(448, 64), 0, r, :] = qs[pl.ds(448, 64), 0, r, :] + added
        return carry

    @pl.when(t == CHUNKS)
    def _():
        lax.fori_loop(0, 4, pair, 0)
        if not last:
            for ref, place in ((sb, 64), (sbh[0], 32), (sbh[1], 32), (cs[0], 0), (cs[1], 0)):
                ref[place] = zero

    upper_open = row < jnp.where(rad < nr - 1, 8, 7)
    lower_open = row >= jnp.where(rad > 0, 0, 1)

    def plane(u, carry):
        s, local = lax.rem(u, 2), u // 2
        i = thick * (t - CHUNKS) + local
        base = 64 * i
        g_r, g_c = geom[1, s], geom[2, s]
        after, before = c_dir[1], c_dir[0]
        for j in range(8):
            v = [ps[base + 8 * j + k, s] for k in range(8)]
            old = [qs[base + 8 * j + k, s] for k in range(8)]
            w = line_apply(v)
            place = 64 * s + 8 * i + j
            nxt = jnp.where(
                lane == 127, pltpu.roll(after, 127 - place, 1), pltpu.roll(v[0], 127, 1)
            )
            prv = jnp.where(
                lane == 0,
                pltpu.roll(before, lax.rem(128 - place, 128), 1),
                pltpu.roll(v[7], 1, 1),
            )
            new = [old[k] + g_c * w[k] for k in range(8)]
            new[7] = new[7] + (v[7] - nxt)
            new[0] = new[0] - (prv - v[0])
            for k in range(8):
                qs[base + 8 * j + k, s] = new[k]
        pq, rq, qq = zero, zero, zero
        for k in range(8):
            v = [ps[base + 8 * j + k, s] for j in range(8)]
            old = [qs[base + 8 * j + k, s] for j in range(8)]
            if not first:
                r = [rs[base + 8 * j + k, s] for j in range(8)]
            w = line_apply(v)
            above = h_dir[16 + 8 * s + i, pl.ds(k, 1), :]
            below = h_dir[8 * s + i, pl.ds(k, 1), :]
            nxt = jnp.where(row == 7, above, pltpu.roll(v[0], 7, 0))
            prv = jnp.where(row == 0, below, pltpu.roll(v[7], 1, 0))
            new = [old[j] + g_r * w[j] for j in range(8)]
            new[7] = new[7] + jnp.where(upper_open, v[7] - nxt, 0.0)
            new[0] = new[0] - jnp.where(lower_open, prv - v[0], 0.0)
            for j in range(8):
                qout[local, 8 * j + k, s] = new[j]
            pq = pq + sum(v[j] * new[j] for j in range(8))
            qq = qq + sum(new[j] * new[j] for j in range(8))
            if not first:
                rq = rq + sum(r[j] * new[j] for j in range(8))
            if not last:
                hs[0][8 * s + i, pl.ds(k, 1), :] = new[7][7:8, :]
                hs[1][8 * s + i, pl.ds(k, 1), :] = new[0][0:1, :]
                for j in range(8):
                    place = 64 * s + 8 * i + j
                    if k == 7:
                        moved = pltpu.roll(new[j], lax.rem(place + 1, 128), 1)
                        cs[0][0] = jnp.where(lane == place, moved, cs[0][0])
                    if k == 0:
                        moved = pltpu.roll(new[j], place, 1)
                        cs[1][0] = jnp.where(lane == place, moved, cs[1][0])
        sums[0] = sums[0] + pq
        sums[1] = sums[1] + (pq if first else rq)
        sums[2] = sums[2] + qq
        return carry

    @pl.when(t >= CHUNKS)
    def _():
        lax.fori_loop(0, 2 * thick, plane, 0)

    if not last:

        @pl.when(t == CHUNKS)
        def _():
            pack_face(lambda n: qout[0, n, 1], sb, sbh)

        @pl.when(t == CHUNKS + PLANES - 1)
        def _():
            pack_face(lambda n: qout[thick - 1, n, 0], sa, sah)

    @pl.when(t == CHUNKS + PLANES - 1)
    def _():
        tile = zero
        for n in range(4):
            tile = jnp.where(row == n, jnp.sum(sums[n], axis=0, keepdims=True), tile)
        part[...] = tile


def stepped(first, last, nr, offset, rold, cf, geom, weights, received, *rest):
    field = struct(*rold.shape)
    span, thick = 64 // CHUNKS, 8 // PLANES
    lines = pl.BlockSpec(
        (8, span) + rold.shape[2:], lambda t: (0, jnp.minimum(t, CHUNKS - 1), 0, 0, 0)
    )
    planes = pl.BlockSpec(
        (thick,) + rold.shape[1:], lambda t: (jnp.maximum(t - CHUNKS, 0), 0, 0, 0, 0)
    )
    outs = [field, struct(8, 128)] + ([struct(2, 8, 128)] if first else [field])
    specs = [planes, VMEM] + ([VMEM] if first else [lines])
    if not (first or last):
        outs.append(field)
        specs.append(lines)
    small = [struct(KEPT, 8, 128)] + ([] if last else [struct(SENT, 8, 128)])
    outs += small
    specs += [VMEM] * len(small)
    args = [offset, rold, cf, geom, weights, received, *rest]
    ins = [SMEM, lines, lines] + [VMEM] * (len(args) - 3)
    if not first:
        ins[7] = ins[8] = lines
    whole = pltpu.VMEM((512,) + rold.shape[2:], F32)
    return pl.pallas_call(
        functools.partial(step, first, last, nr),
        grid=(CHUNKS + PLANES,),
        out_shape=outs,
        in_specs=ins,
        out_specs=specs,
        scratch_shapes=[whole, whole, pltpu.VMEM((4, 8, 128), F32)] + ([] if first else [whole]),
        compiler_params=pltpu.CompilerParams(vmem_limit_bytes=LIMIT * 1024 * 1024),
    )(*args)


LIMIT = 54


def finish(r0, r1, r2, q, c, x_out, r_out):
    c0, c1, c2 = (c[n] for n in range(3))

    def body(n, carry):
        for s in range(2):
            last = r2[0, n, s]
            x_out[0, n, s] = c0 * r0[0, n, s] + c1 * r1[0, n, s] + c2 * last
            r_out[0, n, s] = last - c2 * q[0, n, s]
        return carry

    lax.fori_loop(0, 64, body, 0, unroll=8)


def finished(r0, r1, r2, q, c):
    block = pl.BlockSpec((1,) + r0.shape[1:], lambda n: (n, 0, 0, 0, 0))
    return pl.pallas_call(
        finish,
        grid=(r0.shape[0],),
        out_shape=[jax.ShapeDtypeStruct(r0.shape, F32)] * 2,
        in_specs=[block] * 4 + [VMEM],
        out_specs=[block] * 2,
        compiler_params=pltpu.CompilerParams(vmem_limit_bytes=LIMIT * 1024 * 1024),
    )(r0, r1, r2, q, c)


HOPS = None


def on_device(nb, nr, right_side, coefficient, geometry, interp, face_map, offset):
    cells = nb * right_side.shape[3]
    rotation = lax.rem(offset[0], cells)
    hops = lax.rem((rotation + 64) // 128, nb)

    ways = 2 * hops + (lax.rem(rotation + 64, 128) > 64).astype(jnp.int32)

    def swap(sent):
        if HOPS is None:
            branches = [
                functools.partial(exchanged, nb, nr, hop, up)
                for hop in range(nb)
                for up in (False, True)
            ]
            return lax.switch(ways, branches, sent)
        return exchanged(nb, nr, *HOPS, sent)

    shape = right_side.shape
    cut = (8, 64) + shape[1:]
    right_side, coefficient = right_side.reshape(cut), coefficient.reshape(cut)
    sent, weights = opened(right_side, face_map, interp)
    got = swap(sent)
    q, part, maps, kept, sent = stepped(
        True, False, nr, offset, right_side, coefficient, geometry, weights, got, face_map
    )
    residuals = [right_side]
    p = right_side
    factors = []
    for it in range(1, ITERS):
        last = it == ITERS - 1
        factors.append(reduced(nb, nr, part))
        got = swap(sent)
        q, part, r, *rest = stepped(
            False,
            last,
            nr,
            offset,
            residuals[-1],
            coefficient,
            geometry,
            weights,
            got,
            factors[-1],
            p,
            q,
            maps,
            kept,
        )
        if not last:
            p, kept, sent = rest
        residuals.append(r)
    factors.append(reduced(nb, nr, part))
    (a0, b0), (a1, b1), (a2, _) = factors
    one = a1 + b1 * a2
    weighed = jnp.stack([a0 + b0 * one, one, a2])
    return tuple(x.reshape(shape) for x in finished(*residuals, q, weighed))


def solution(mesh):
    nb, nr = mesh.shape["blk"], mesh.shape["rad"]
    field = P(None, None, "rad", "blk")
    return jax.shard_map(
        functools.partial(on_device, nb, nr),
        mesh=mesh,
        in_specs=(field, field, field, P(), P("rad", "blk"), P()),
        out_specs=(field, field),
        check_vma=False,
    )
```

```python
import functools

import jax
import jax.numpy as jnp
import numpy as np
from jax import lax
from jax.experimental import pallas as pl
from jax.experimental.pallas import tpu as pltpu
from jax.sharding import PartitionSpec as P

ITERS = 3
MESH = pl.DeviceIdType.MESH
F32 = jnp.float32
BF16 = jnp.bfloat16


def stiffness_halves():
    n = np.arange(8)
    x = -np.cos(np.pi * n / 7.0)
    c = np.where((n == 0) | (n == 7), 2.0, 1.0)
    sign = 1.0 - 2.0 * ((n[:, None] + n[None, :]) % 2)
    gap = x[:, None] - x[None, :] + np.eye(8)
    d = (c[:, None] / c[None, :]) * sign / gap * (1.0 - np.eye(8))
    d = d - np.diag(d.sum(axis=1))
    k = d.T @ d
    mirror = k[:4, ::-1][:, :4]
    return 0.5 * (k[:4, :4] + mirror), 0.5 * (k[:4, :4] - mirror)


EVEN, ODD = stiffness_halves()


def line_apply(v):
    sums = [v[m] + v[7 - m] for m in range(4)]
    diffs = [v[m] - v[7 - m] for m in range(4)]
    out = [None] * 8
    for m in range(4):
        e = sums[0] * float(EVEN[m, 0])
        o = diffs[0] * float(ODD[m, 0])
        for n in range(1, 4):
            e = e + sums[n] * float(EVEN[m, n])
            o = o + diffs[n] * float(ODD[m, n])
        out[m] = e + o
        out[7 - m] = e - o
    return out


def split_rows(a):
    high = a.astype(BF16)
    low = (a - high.astype(F32)).astype(BF16)
    return jnp.concatenate([high, low, high, low], axis=0)


def split_columns(p):
    both = jnp.concatenate([p, p], axis=1)
    high = both.astype(BF16)
    low = (both - high.astype(F32)).astype(BF16)
    return jnp.concatenate([high, low], axis=1)


def choose(blocks, which):
    which = jnp.broadcast_to(which, (64, 128))
    out = blocks[0:64]
    for m in range(1, 4):
        out = jnp.where(which == float(m), blocks[64 * m : 64 * m + 64], out)
    return out


VMEM = pl.BlockSpec(memory_space=pltpu.VMEM)
SMEM = pl.BlockSpec(memory_space=pltpu.SMEM)
EDGE = pl.BlockSpec(memory_space=pl.ANY)


def struct(*shape):
    return jax.ShapeDtypeStruct(shape, F32)


def lanes():
    return lax.broadcasted_iota(jnp.int32, (8, 128), 1)


def rows():
    return lax.broadcasted_iota(jnp.int32, (8, 128), 0)


def pack_face(read, full, half):
    lane = lanes()

    def body(n, carry):
        one, two = read(n), read(n + 32)
        full[n] = one
        full[n + 32] = two
        half[0][n] = jnp.where(lane < 64, one, pltpu.roll(two, 64, 1))
        half[1][n] = jnp.where(lane < 64, pltpu.roll(one, 64, 1), two)
        return carry

    lax.fori_loop(0, 32, body, 0)


def pack_halos(read, hs, cs):
    lane = lanes()
    zero = jnp.zeros((8, 128), F32)

    def body(n, carry):
        upper, lower = carry
        side, i = n // 8, lax.rem(n, 8)
        for k in range(8):
            hs[0][n, pl.ds(k, 1), :] = read(64 * i + 56 + k, side)[7:8, :]
            hs[1][n, pl.ds(k, 1), :] = read(64 * i + k, side)[0:1, :]
        for j in range(8):
            place = 8 * n + j
            last = pltpu.roll(read(64 * i + 8 * j + 7, side), lax.rem(place + 1, 128), 1)
            first = pltpu.roll(read(64 * i + 8 * j, side), place, 1)
            upper = jnp.where(lane == place, last, upper)
            lower = jnp.where(lane == place, first, lower)
        return upper, lower

    upper, lower = lax.fori_loop(0, 16, body, (zero, zero))
    cs[0][0] = upper
    cs[1][0] = lower


def turn(main, near, by):
    lane = lanes()
    first = jnp.where(by > 0, 128 - by, 0)
    end = jnp.where(by > 0, 128, -by)
    missing = jnp.logical_and(lane >= first, lane < end)
    picked = jnp.where(missing, near, main)
    return pltpu.roll(picked, lax.rem(by + 128, 128), 1)


SENT = 296
KEPT = 328


def sent_parts(ref):
    part = lambda first, count: ref.at[pl.ds(first, count)]
    return (
        part(0, 64),
        (part(64, 32), part(96, 32)),
        part(128, 65),
        (part(193, 33), part(226, 33)),
        (part(259, 16), part(275, 16)),
        (part(291, 1), part(292, 1)),
    )


def kept_parts(ref):
    part = lambda first, count: ref.at[pl.ds(first, count)]
    return [part(64 * n, 64) for n in range(4)] + [
        part(256, 32),
        part(288, 32),
        part(320, 2),
        part(322, 2),
    ]


def opening(rhs, face_map, interp, sent, weights):
    sa, sah, sb, sbh, hs, cs = sent_parts(sent)
    pack_face(lambda n: rhs[7, n, 0], sa, sah)
    pack_face(lambda n: rhs[0, n, 1], sb, sbh)
    which = face_map[...].astype(F32)
    sb[64] = which
    sbh[0][32] = which
    sbh[1][32] = which
    pack_halos(lambda n, side: rhs[n // 64, lax.rem(n, 64), side], hs, cs)
    blocks = interp[...]
    weights[0] = split_columns(blocks.reshape(256, 64))
    turned = jnp.concatenate(
        [
            jnp.concatenate([blocks[0], blocks[1]], axis=1).T,
            jnp.concatenate([blocks[2], blocks[3]], axis=1).T,
        ],
        axis=0,
    )
    weights[1] = split_columns(turned)


def opened(right_side, face_map, interp):
    return pl.pallas_call(
        opening,
        out_shape=[struct(SENT, 8, 128), jax.ShapeDtypeStruct((2, 256, 256), BF16)],
        in_specs=[VMEM] * 3,
        out_specs=[VMEM] * 2,
        compiler_params=pltpu.CompilerParams(vmem_limit_bytes=LIMIT * 1024 * 1024),
    )(right_side, face_map, interp)


def exchange(nb, nr, hop, sent, got, send_sem, recv_sem):
    blk = lax.axis_index("blk")
    rad = lax.axis_index("rad")

    def along(by):
        return {"blk": lax.rem(blk + by + 2 * nb, nb), "rad": rad}

    def across(by):
        return {"blk": blk, "rad": lax.rem(rad + by + nr, nr)}

    sa, sah, sb, sbh, hs, cs = sent_parts(sent)
    ra, rah, rb, rbh, hrecv, crecv = sent_parts(got)
    plan = []
    for src, half, dst, dhalf, way in ((sa, sah, ra, rah, 1), (sb, sbh, rb, rbh, -1)):
        for source, target, by in (
            (src, dst, way * hop),
            (half[0], dhalf[0], way * hop - 1),
            (half[1], dhalf[1], way * hop + 1),
        ):
            plan.append((source, target, along(by) if by % nb else None))
    plan += [
        (hs[0], hrecv[0], across(1)),
        (hs[1], hrecv[1], across(-1)),
        (cs[0], crecv[0], along(1)),
        (cs[1], crecv[1], along(-1)),
    ]
    peers = [peer for _, _, peer in plan if peer is not None]
    barrier = pltpu.get_barrier_semaphore()
    for peer in peers:
        pl.semaphore_signal(barrier, inc=1, device_id=peer, device_id_type=MESH)
    pl.semaphore_wait(barrier, len(peers))
    copies = []
    for n, (source, target, peer) in enumerate(plan):
        if peer is None:
            copy = pltpu.make_async_copy(source, target, recv_sem.at[n])
        else:
            copy = pltpu.make_async_remote_copy(
                source,
                target,
                send_sem.at[n],
                recv_sem.at[n],
                device_id=peer,
                device_id_type=MESH,
            )
        copy.start()
        copies.append(copy)
    for copy in copies:
        copy.wait()


def exchanged(nb, nr, hop, sent):
    return pl.pallas_call(
        functools.partial(exchange, nb, nr, hop),
        out_shape=struct(*sent.shape),
        in_specs=[EDGE],
        out_specs=EDGE,
        scratch_shapes=[pltpu.SemaphoreType.DMA((10,)), pltpu.SemaphoreType.DMA((10,))],
        compiler_params=pltpu.CompilerParams(
            collective_id=hop,
            has_side_effects=True,
            vmem_limit_bytes=LIMIT * 1024 * 1024,
        ),
    )(sent)


def reduce_kernel(nb, nr, part, scal, source, one, two, send_sem, recv_sem):
    blk = lax.axis_index("blk")
    rad = lax.axis_index("rad")

    def plane_peer(d):
        return {"blk": (blk // 16) * 16 + lax.rem(lax.rem(blk, 16) + d, 16), "rad": rad}

    def line_peer(d):
        place = lax.rem((blk // 16) * nr + rad + d, 2 * nr)
        return {"blk": (place // nr) * 16 + lax.rem(blk, 16), "rad": lax.rem(place, nr)}

    stages = (
        (16, lax.rem(blk, 16), plane_peer, one),
        (2 * nr, (blk // 16) * nr + rad, line_peer, two),
    )
    barrier = pltpu.get_barrier_semaphore()
    for count, _, peer, _ in stages:
        for d in range(1, count):
            pl.semaphore_signal(barrier, inc=1, device_id=peer(d), device_id_type=MESH)
    pl.semaphore_wait(barrier, 14 + 2 * nr)
    tile = part[...]
    for stage, (count, place, peer, buf) in enumerate(stages):
        source[stage] = tile
        buf[place] = tile
        for d in range(1, count):
            pltpu.make_async_remote_copy(
                source.at[stage],
                buf.at[place],
                send_sem.at[stage],
                recv_sem.at[stage],
                device_id=peer(d),
                device_id_type=MESH,
            ).start()
        whole = buf.at[pl.ds(0, count - 1)]
        pltpu.make_async_copy(whole, whole, recv_sem.at[stage]).wait()
        tile = buf[0]
        for n in range(1, count):
            tile = tile + buf[n]
        pltpu.make_async_copy(whole, whole, send_sem.at[stage]).wait()
    totals = jnp.sum(tile, axis=1, keepdims=True)
    pq, rq, qq, rr = [jnp.broadcast_to(totals[n : n + 1], (8, 128)) for n in range(4)]
    alpha = rr / pq
    fresh = rr - 2.0 * alpha * rq + alpha * alpha * qq
    scal[0] = alpha
    scal[1] = fresh / rr


def reduced(nb, nr, part):
    return pl.pallas_call(
        functools.partial(reduce_kernel, nb, nr),
        out_shape=struct(2, 8, 128),
        in_specs=[VMEM],
        out_specs=VMEM,
        scratch_shapes=[
            pltpu.VMEM((2, 8, 128), F32),
            pltpu.VMEM((16, 8, 128), F32),
            pltpu.VMEM((2 * nr, 8, 128), F32),
            pltpu.SemaphoreType.DMA((2,)),
            pltpu.SemaphoreType.DMA((2,)),
        ],
        compiler_params=pltpu.CompilerParams(
            collective_id=nb, has_side_effects=True, vmem_limit_bytes=LIMIT * 1024 * 1024
        ),
    )(part)


CHUNKS = 4
PLANES = 4


def step(first, last, nr, *refs):
    refs = list(refs)
    take = lambda n: [refs.pop(0) for _ in range(n)]
    offset, rold, cf, geom, weights = take(5)
    (got,) = take(1)
    ra, rah, rb, rbh, hrecv, crecv = sent_parts(got)
    if first:
        (face_map,) = take(1)
        alpha = beta = None
    else:
        scal, pold, qold, maps = take(4)
        olds = kept_parts(take(1)[0])
        alpha, beta = scal[0], scal[1]
    qout, part = take(2)
    if first:
        (maps,) = take(1)
    else:
        (rout,) = take(1)
    if not (first or last):
        (pout,) = take(1)
    news = kept_parts(take(1)[0])
    if not last:
        sa, sah, sb, sbh, hs, cs = sent_parts(take(1)[0])
    ps, qs, sums = take(3)
    rs = ps if first else take(1)[0]
    t = pl.program_id(0)
    rad = lax.axis_index("rad")
    lane, row = lanes(), rows()
    zero = jnp.zeros((8, 128), F32)
    shift = lax.rem(offset[0] + 64, 128) - 64
    a_res, a_dir, b_res, b_dir, h_res, h_dir, c_res, c_dir = news
    span = 64 // CHUNKS
    thick = 8 // PLANES

    @pl.when(t == 0)
    def _():
        for n in range(4):
            sums[n] = zero
        if first:
            maps[0] = face_map[...].astype(F32)
            maps[1] = turn(rb[64], jnp.where(lane < 64, rbh[0][32], rbh[1][32]), -shift)

    def refresh(slot, place, fresh):
        res, ahead = news[slot], news[slot + 1]
        if first:
            res[place] = fresh
            ahead[place] = fresh
        else:
            value = olds[slot][place] - alpha * fresh
            res[place] = value
            ahead[place] = value + beta * olds[slot + 1][place]

    def columns(u, total):
        line = span * t + u
        for s in range(2):
            r = [rold[i, u, s] for i in range(8)]
            if first:
                v = r
            else:
                q = [qold[i, u, s] for i in range(8)]
                p = [pold[i, u, s] for i in range(8)]
                r = [r[i] - alpha * q[i] for i in range(8)]
                v = [r[i] + beta * p[i] for i in range(8)]
            c = [cf[i, u, s] for i in range(8)]
            g = geom[0, s]
            w = line_apply(v)
            squares = [x * x for x in r]
            squares = [squares[n] + squares[n + 4] for n in range(4)]
            total = total + ((squares[0] + squares[1]) + (squares[2] + squares[3]))
            for i in range(8):
                n = 64 * i + line
                ps[n, s] = v[i]
                if not first:
                    rs[n, s] = r[i]
                    rout[i, u, s] = r[i]
                    if not last:
                        pout[i, u, s] = v[i]
                qs[n, s] = c[i] * v[i] + g * w[i]
        return total

    @pl.when(t < CHUNKS)
    def _():
        sums[3] = sums[3] + lax.fori_loop(0, span, columns, zero)

    def halo_step(n, carry):
        for side in range(2):
            refresh(4, 16 * side + n, hrecv[side][n])
        return carry

    def face_step(n, carry):
        for main, half, slot, by in ((ra, rah, 0, shift), (rb, rbh, 2, -shift)):
            low, high = half[0][n], half[1][n]
            mixed = pltpu.roll(jnp.where(lane < 64, high, low), 64, 1)
            nears = (jnp.where(lane < 64, low, mixed), jnp.where(lane < 64, mixed, high))
            for place, near in zip((n, n + 32), nears):
                refresh(slot, place, turn(main[place], near, by))
        return carry

    def pair(half, carry):
        jumps = []
        here = []
        for u in range(2):
            r = 2 * half + u
            own = ps[pl.ds(448, 64), 0, r, :]
            over = a_dir[:, r, :]
            mapped = jnp.dot(
                weights[0],
                split_rows(jnp.concatenate([own, over], axis=1)),
                preferred_element_type=F32,
            )
            mine = maps[1, pl.ds(r, 1), :]
            theirs = maps[0, pl.ds(r, 1), :]
            jumps.append(choose(mapped[:, :128], mine) - b_dir[:, r, :])
            here.append(mine)
            jump = choose(mapped[:, 128:], theirs) - ps[pl.ds(0, 64), 1, r, :]
            qs[pl.ds(0, 64), 1, r, :] = qs[pl.ds(0, 64), 1, r, :] - jump
        back = jnp.dot(
            weights[1],
            split_rows(jnp.concatenate(jumps, axis=1)),
            preferred_element_type=F32,
        )
        for u in range(2):
            r = 2 * half + u
            added = choose(back[:, 128 * u : 128 * u + 128], here[u])
            qs[pl.ds(448, 64), 0, r, :] = qs[pl.ds(448, 64), 0, r, :] + added
        return carry

    @pl.when(t == CHUNKS)
    def _():
        lax.fori_loop(0, 16, halo_step, 0)
        for side in range(2):
            refresh(6, side, crecv[side][0])
        lax.fori_loop(0, 32, face_step, 0)
        lax.fori_loop(0, 4, pair, 0)
        if not last:
            for ref, place in ((sb, 64), (sbh[0], 32), (sbh[1], 32), (cs[0], 0), (cs[1], 0)):
                ref[place] = zero

    upper_open = row < jnp.where(rad < nr - 1, 8, 7)
    lower_open = row >= jnp.where(rad > 0, 0, 1)

    def plane(u, carry):
        s, local = lax.rem(u, 2), u // 2
        i = thick * (t - CHUNKS) + local
        base = 64 * i
        g_r, g_c = geom[1, s], geom[2, s]
        after, before = c_dir[1], c_dir[0]
        for j in range(8):
            v = [ps[base + 8 * j + k, s] for k in range(8)]
            old = [qs[base + 8 * j + k, s] for k in range(8)]
            w = line_apply(v)
            place = 64 * s + 8 * i + j
            nxt = jnp.where(
                lane == 127, pltpu.roll(after, 127 - place, 1), pltpu.roll(v[0], 127, 1)
            )
            prv = jnp.where(
                lane == 0,
                pltpu.roll(before, lax.rem(128 - place, 128), 1),
                pltpu.roll(v[7], 1, 1),
            )
            new = [old[k] + g_c * w[k] for k in range(8)]
            new[7] = new[7] + (v[7] - nxt)
            new[0] = new[0] - (prv - v[0])
            for k in range(8):
                qs[base + 8 * j + k, s] = new[k]
        pq, rq, qq = zero, zero, zero
        for k in range(8):
            v = [ps[base + 8 * j + k, s] for j in range(8)]
            old = [qs[base + 8 * j + k, s] for j in range(8)]
            if not first:
                r = [rs[base + 8 * j + k, s] for j in range(8)]
            w = line_apply(v)
            above = h_dir[16 + 8 * s + i, pl.ds(k, 1), :]
            below = h_dir[8 * s + i, pl.ds(k, 1), :]
            nxt = jnp.where(row == 7, above, pltpu.roll(v[0], 7, 0))
            prv = jnp.where(row == 0, below, pltpu.roll(v[7], 1, 0))
            new = [old[j] + g_r * w[j] for j in range(8)]
            new[7] = new[7] + jnp.where(upper_open, v[7] - nxt, 0.0)
            new[0] = new[0] - jnp.where(lower_open, prv - v[0], 0.0)
            for j in range(8):
                qout[local, 8 * j + k, s] = new[j]
            pq = pq + sum(v[j] * new[j] for j in range(8))
            qq = qq + sum(new[j] * new[j] for j in range(8))
            if not first:
                rq = rq + sum(r[j] * new[j] for j in range(8))
            if not last:
                hs[0][8 * s + i, pl.ds(k, 1), :] = new[7][7:8, :]
                hs[1][8 * s + i, pl.ds(k, 1), :] = new[0][0:1, :]
                for j in range(8):
                    place = 64 * s + 8 * i + j
                    if k == 7:
                        moved = pltpu.roll(new[j], lax.rem(place + 1, 128), 1)
                        cs[0][0] = jnp.where(lane == place, moved, cs[0][0])
                    if k == 0:
                        moved = pltpu.roll(new[j], place, 1)
                        cs[1][0] = jnp.where(lane == place, moved, cs[1][0])
        sums[0] = sums[0] + pq
        sums[1] = sums[1] + (pq if first else rq)
        sums[2] = sums[2] + qq
        return carry

    @pl.when(t >= CHUNKS)
    def _():
        lax.fori_loop(0, 2 * thick, plane, 0)

    if not last:

        @pl.when(t == CHUNKS)
        def _():
            pack_face(lambda n: qout[0, n, 1], sb, sbh)

        @pl.when(t == CHUNKS + PLANES - 1)
        def _():
            pack_face(lambda n: qout[thick - 1, n, 0], sa, sah)

    @pl.when(t == CHUNKS + PLANES - 1)
    def _():
        tile = zero
        for n in range(4):
            tile = jnp.where(row == n, jnp.sum(sums[n], axis=0, keepdims=True), tile)
        part[...] = tile


def stepped(first, last, nr, offset, rold, cf, geom, weights, received, *rest):
    field = struct(*rold.shape)
    span, thick = 64 // CHUNKS, 8 // PLANES
    lines = pl.BlockSpec(
        (8, span) + rold.shape[2:], lambda t: (0, jnp.minimum(t, CHUNKS - 1), 0, 0, 0)
    )
    planes = pl.BlockSpec(
        (thick,) + rold.shape[1:], lambda t: (jnp.maximum(t - CHUNKS, 0), 0, 0, 0, 0)
    )
    outs = [field, struct(8, 128)] + ([struct(2, 8, 128)] if first else [field])
    specs = [planes, VMEM] + ([VMEM] if first else [lines])
    if not (first or last):
        outs.append(field)
        specs.append(lines)
    small = [struct(KEPT, 8, 128)] + ([] if last else [struct(SENT, 8, 128)])
    outs += small
    specs += [VMEM] * len(small)
    args = [offset, rold, cf, geom, weights, received, *rest]
    ins = [SMEM, lines, lines] + [VMEM] * (len(args) - 3)
    if not first:
        ins[7] = ins[8] = lines
    whole = pltpu.VMEM((512,) + rold.shape[2:], F32)
    return pl.pallas_call(
        functools.partial(step, first, last, nr),
        grid=(CHUNKS + PLANES,),
        out_shape=outs,
        in_specs=ins,
        out_specs=specs,
        scratch_shapes=[whole, whole, pltpu.VMEM((4, 8, 128), F32)] + ([] if first else [whole]),
        compiler_params=pltpu.CompilerParams(vmem_limit_bytes=LIMIT * 1024 * 1024),
    )(*args)


LIMIT = 54


def finish(r0, r1, r2, q, c, x_out, r_out):
    c0, c1, c2 = (c[n] for n in range(3))

    def body(n, carry):
        for s in range(2):
            last = r2[0, n, s]
            x_out[0, n, s] = c0 * r0[0, n, s] + c1 * r1[0, n, s] + c2 * last
            r_out[0, n, s] = last - c2 * q[0, n, s]
        return carry

    lax.fori_loop(0, 64, body, 0, unroll=8)


def finished(r0, r1, r2, q, c):
    block = pl.BlockSpec((1,) + r0.shape[1:], lambda n: (n, 0, 0, 0, 0))
    return pl.pallas_call(
        finish,
        grid=(r0.shape[0],),
        out_shape=[jax.ShapeDtypeStruct(r0.shape, F32)] * 2,
        in_specs=[block] * 4 + [VMEM],
        out_specs=[block] * 2,
        compiler_params=pltpu.CompilerParams(vmem_limit_bytes=LIMIT * 1024 * 1024),
    )(r0, r1, r2, q, c)


HOPS = None


def on_device(nb, nr, right_side, coefficient, geometry, interp, face_map, offset):
    cells = nb * right_side.shape[3]
    rotation = lax.rem(offset[0], cells)
    hops = lax.rem((rotation + 64) // 128, nb)

    def swap(sent):
        if HOPS is None:
            branches = [functools.partial(exchanged, nb, nr, hop) for hop in range(nb)]
            return lax.switch(hops, branches, sent)
        return exchanged(nb, nr, HOPS, sent)

    shape = right_side.shape
    cut = (8, 64) + shape[1:]
    right_side, coefficient = right_side.reshape(cut), coefficient.reshape(cut)
    sent, weights = opened(right_side, face_map, interp)
    got = swap(sent)
    q, part, maps, kept, sent = stepped(
        True, False, nr, offset, right_side, coefficient, geometry, weights, got, face_map
    )
    residuals = [right_side]
    p = right_side
    factors = []
    for it in range(1, ITERS):
        last = it == ITERS - 1
        factors.append(reduced(nb, nr, part))
        got = swap(sent)
        q, part, r, *rest = stepped(
            False,
            last,
            nr,
            offset,
            residuals[-1],
            coefficient,
            geometry,
            weights,
            got,
            factors[-1],
            p,
            q,
            maps,
            kept,
        )
        if not last:
            p, kept, sent = rest
        residuals.append(r)
    factors.append(reduced(nb, nr, part))
    (a0, b0), (a1, b1), (a2, _) = factors
    one = a1 + b1 * a2
    weighed = jnp.stack([a0 + b0 * one, one, a2])
    return tuple(x.reshape(shape) for x in finished(*residuals, q, weighed))


def solution(mesh):
    nb, nr = mesh.shape["blk"], mesh.shape["rad"]
    field = P(None, None, "rad", "blk")
    return jax.shard_map(
        functools.partial(on_device, nb, nr),
        mesh=mesh,
        in_specs=(field, field, field, P(), P("rad", "blk"), P()),
        out_specs=(field, field),
        check_vma=False,
    )
```
